1024 devices in a mesh: dp: 64 (over z, y), head: 16 (over x, core).
Axes of the slice: x: 8, y: 8, z: 8, core: 2. Of those that a mesh axis runs over, the one named last changes fastest.
Arguments:
- latent: bfloat16 [98304, 512], P('dp', 'head'), may hold values from -16 to 16
- value_grad: bfloat16 [98304, 8192], P('dp', 'head'), may hold values from -6 to 6
- lengths: int32 [64], replicated, may hold values from 1 to 1536, 32768 in all
Outputs:
- update: bfloat16 [64, 512, 128], P('head')
The draws below stay inside these ranges and needn't reach their ends.
Inputs may be any that keep to these rules, and one draw needn't show every extreme that they name: The lengths sum to 32768; the longest is exactly 1536.
All inputs are finite; a program needn't handle non-finite values.
Results may differ from the reference program's by a relative error of at most 0.035.
Values may be sent and summed in bfloat16 or wider, within the bound.
No kernel may reach another device: no remote copies, remote signals or barrier semaphores. Data moves between devices by JAX's collectives and lax.ppermute only.
A program may use at most 32 MiB of HBM per device.

```python
import math
import jax
import jax.numpy as jnp
import numpy as np
from jax import lax

KV_RANK = 512
V_DIM = 128
HEADS = 64
MEAN_LEN = 512
ITERS = 5
CAP = 1536
ROWS = 98304
N_DP = 64


def strengthened(values, rng, source, target, blocks, factor):
    def block_of(axis_at):
        return (jnp.arange(values.shape[axis_at]) // (values.shape[axis_at] // blocks)).reshape((-1,) + (1,) * (values.ndim - 1 - axis_at))

    first = jax.random.permutation(rng, blocks)[block_of(target)]
    second = (block_of(target) + blocks // 2) % blocks
    return jnp.where((block_of(source) == first) | (block_of(source) == second), factor * values, values)


def levels(stream_key, shape, shards, smallest, largest):
    factor_of, own = 1.0, jax.random.fold_in(stream_key, 6)
    for axis_at, shards_of in shards:
        draws = jnp.exp(jax.random.uniform(jax.random.fold_in(own, axis_at), (shards_of,), jnp.float32, smallest / len(shards), largest / len(shards)))
        factor_of = factor_of * jnp.repeat(draws, shape[axis_at] // shards_of).reshape([-1 if axis == axis_at else 1 for axis in range(len(shape))])
    return factor_of


def profile(amount, total, most, lean):
    portions = [(1 << 20) // math.isqrt(standing ** lean) + 1 for standing in range(2, amount + 1)]
    spare, counts = total - most - (amount - 1), [1] * (amount - 1)
    while spare > 0:
        candidates = [i for i in range(amount - 1) if counts[i] < most]
        pool, budget = sum([portions[i] for i in candidates]), spare
        for i in candidates:
            addition = min(most - counts[i], max(1, budget * portions[i] // pool), spare)
            counts[i] = counts[i] + addition
            spare = spare - addition
    return np.array([most] + counts)


def ragged_sizes(stream_key, amount, total, most, slope):
    if amount == 2:
        one = jax.random.randint(stream_key, (), max(1, total - most), min(most, total - 1) + 1)
        return jnp.stack([one, total - one])
    sizes = jnp.asarray(profile(amount, total, most, slope), jnp.int32)
    twos = (amount - 1) // 2
    donor, receiver = sizes[1:1 + 2 * twos:2], sizes[2:2 + 2 * twos:2]
    slack = jnp.minimum(donor - 1, most - receiver)
    shifted = jax.random.randint(jax.random.fold_in(stream_key, 1), (twos,), 0, 1 << 20) % (slack + 1)
    sizes = sizes.at[1:1 + 2 * twos:2].set(donor - shifted).at[2:2 + 2 * twos:2].set(receiver + shifted)
    return sizes[jax.random.permutation(jax.random.fold_in(stream_key, 2), amount)]


def normal_values(stream_key, extent, width, limit, shards=(), kind=jnp.bfloat16):
    values = width * jax.random.normal(stream_key, extent, jnp.float32)
    if shards:
        values = values * levels(stream_key, extent, shards, -0.22, 0.18)
    return jnp.clip(values, -limit, limit).astype(kind)


def heavy_noise(own_key, shape, width, bound, pieces, heavy, held_as=jnp.bfloat16):
    drawn = width * jax.random.normal(own_key, shape, jnp.float32)
    if pieces:
        drawn = drawn * levels(own_key, shape, pieces, -0.22, 0.18)
    return jnp.clip(strengthened(drawn, jax.random.fold_in(own_key, 3), *heavy), -bound, bound).astype(held_as)


def setup_inputs(seed: int = 0) -> dict:
    seeds = jax.random.split(jax.random.key(seed), 4)
    latent = heavy_noise(seeds[0], (ROWS, KV_RANK), 1.0, 16.0, ((0, 64), (1, 16)), (0, 1, 64, 4.0))
    value_grad = normal_values(seeds[1], (ROWS, HEADS * V_DIM), 1.0, 6.0, ((0, 64), (1, 16)))
    lengths = ragged_sizes(seeds[2], N_DP, N_DP * MEAN_LEN, CAP, 2).astype(jnp.int32)
    return {"latent": latent, "value_grad": value_grad, "lengths": lengths}


epsilon = 1e-07
coef_one = 3.4445
coef_two = -4.775
coef_three = 2.0315

def newton_schulz(grad_sum):
    split = grad_sum.reshape(KV_RANK, HEADS, V_DIM)
    head_squares = lax.optimization_barrier(jnp.sum(split * split, axis=(0, 2)))
    head_norm = jnp.sqrt(head_squares)
    ortho = (split / (head_norm[None, :, None] + epsilon)).astype(jnp.bfloat16)
    for step in range(ITERS):
        wide = ortho.astype(jnp.float32)
        gram_mat = jnp.einsum('rhv,rhw->hvw', wide, wide, precision=lax.Precision.HIGHEST).astype(jnp.bfloat16)
        gram_wide = gram_mat.astype(jnp.float32)
        squared = jnp.einsum('hvu,huw->hvw', gram_wide, gram_wide, precision=lax.Precision.HIGHEST)
        poly_mat = (coef_two * gram_wide + coef_three * squared).astype(jnp.bfloat16)
        product = jnp.einsum('rhv,hvw->rhw', wide, poly_mat.astype(jnp.float32), precision=lax.Precision.HIGHEST)
        ortho = (coef_one * wide + product).astype(jnp.bfloat16)
    scale = 0.2 * max(KV_RANK, V_DIM) ** 0.5
    update = (scale * ortho.astype(jnp.float32)).astype(jnp.bfloat16)
    return jnp.transpose(update, (1, 0, 2))

def reference(latent, value_grad, lengths):
    row_total = latent.shape[0]
    capacity = row_total // N_DP
    positions = jnp.arange(row_total, dtype=jnp.int32)
    owner_len = jnp.repeat(lengths, capacity)
    live_rows = positions % capacity < owner_len
    masked = jnp.where(live_rows[:, None], value_grad, jnp.zeros_like(value_grad))
    grad_sum = jnp.dot(latent.T, masked, preferred_element_type=jnp.float32)
    return newton_schulz(grad_sum)
```

```python
import jax
import jax.numpy as jnp
from jax import lax
from jax.experimental import pallas as pl
from jax.experimental.pallas import tpu as pltpu
from jax.sharding import Mesh, PartitionSpec as P

KV_RANK = 512
V_DIM = 128
ITERS = 5

epsilon = 1e-07
coef_one = 3.4445
coef_two = -4.775
coef_three = 2.0315

PIECE = 16
NN = (((1,), (0,)), ((), ()))
NT = (((1,), (1,)), ((), ()))


def partial_kernel(lengths_ref, latent_ref, own_ref, other_ref, out_ref):
    own_length = lengths_ref[lax.axis_index(("z", "y"))]
    core = lax.axis_index("c")
    columns, capacity = latent_ref.shape
    slot = lax.broadcasted_iota(jnp.int32, (columns, capacity), 1)
    live = jnp.where(slot < own_length, latent_ref[...], jnp.zeros((), jnp.bfloat16))
    heads = own_ref.shape[1] // V_DIM
    for grad_ref, owner in ((own_ref, core), (other_ref, 1 - core)):
        sums = lax.dot_general(live, grad_ref[...], NN, preferred_element_type=jnp.float32)
        sums = sums.astype(jnp.bfloat16)
        for block in range(columns // PIECE):
            for head in range(heads):
                out_ref[block * heads + head, owner] = sums[
                    block * PIECE : (block + 1) * PIECE, head * V_DIM : (head + 1) * V_DIM
                ]


def total_kernel(parts_ref, out_ref):
    shares = parts_ref.shape[0]
    total = jnp.sum(parts_ref[...].astype(jnp.float32), axis=0).astype(jnp.bfloat16)
    out_ref[...] = jnp.broadcast_to(total[None], (shares,) + total.shape)


def ortho_kernel(sums_ref, out_ref):
    heads = out_ref.shape[0]
    blocks = sums_ref.shape[0] // heads
    cores = sums_ref.shape[1]
    scale = 0.2 * max(KV_RANK, V_DIM) ** 0.5
    halves = 2
    ortho = []
    for head in range(heads):
        rows = [
            sums_ref[(chip * halves + half) * heads + head, core]
            for chip in range(blocks // halves)
            for core in range(cores)
            for half in range(halves)
        ]
        wide = jnp.concatenate(rows, axis=0).astype(jnp.float32)
        norm = jnp.sqrt(jnp.sum(wide * wide))
        wide = wide * (1.0 / (norm + epsilon))
        ortho.append(jnp.transpose(wide).astype(jnp.bfloat16))
    for step in range(ITERS):
        gram = [
            lax.dot_general(x, x, NT, preferred_element_type=jnp.float32).astype(jnp.bfloat16)
            for x in ortho
        ]
        squared = [lax.dot_general(a, a, NN, preferred_element_type=jnp.float32) for a in gram]
        poly = [
            (coef_two * a.astype(jnp.float32) + coef_three * s).astype(jnp.bfloat16)
            for a, s in zip(gram, squared)
        ]
        product = [
            lax.dot_general(b, x, NN, preferred_element_type=jnp.float32)
            for b, x in zip(poly, ortho)
        ]
        ortho = [
            (coef_one * x.astype(jnp.float32) + p).astype(jnp.bfloat16)
            for x, p in zip(ortho, product)
        ]
    for head in range(heads):
        out_ref[head] = jnp.transpose(scale * ortho[head].astype(jnp.float32)).astype(jnp.bfloat16)


def body(latent, value_grad, lengths):
    capacity, lat_cols = latent.shape
    heads = value_grad.shape[1] // V_DIM
    chips, cores, shares = lax.axis_size("x"), lax.axis_size("c"), lax.axis_size(("z", "y"))
    vmem = pl.BlockSpec(memory_space=pltpu.VMEM)
    smem = pl.BlockSpec(memory_space=pltpu.SMEM)

    other_grad = lax.ppermute(value_grad, "c", [(0, 1), (1, 0)])
    spread = jnp.broadcast_to(latent.T[None], (chips, lat_cols, capacity))
    gathered = lax.all_to_all(spread, "x", 0, 0, tiled=True)
    gathered = gathered.reshape(chips * lat_cols, capacity)

    partial = pl.pallas_call(
        partial_kernel,
        out_shape=jax.ShapeDtypeStruct((shares, cores, PIECE, V_DIM), jnp.bfloat16),
        in_specs=[smem, vmem, vmem, vmem],
        out_specs=vmem,
        compiler_params=pltpu.CompilerParams(vmem_limit_bytes=32 * 2**20),
    )(lengths, gathered, value_grad, other_grad)

    parts = lax.all_to_all(
        partial.reshape(shares * cores, PIECE, V_DIM), ("z", "y", "c"), 0, 0, tiled=True
    ).reshape(shares, cores, PIECE, V_DIM)

    total = pl.pallas_call(
        total_kernel,
        out_shape=jax.ShapeDtypeStruct(parts.shape, jnp.bfloat16),
        in_specs=[vmem],
        out_specs=vmem,
        compiler_params=pltpu.CompilerParams(vmem_limit_bytes=32 * 2**20),
    )(parts)

    sums = lax.all_to_all(total, ("z", "y"), 0, 0, tiled=True)

    return pl.pallas_call(
        ortho_kernel,
        out_shape=jax.ShapeDtypeStruct((heads, KV_RANK, V_DIM), jnp.bfloat16),
        in_specs=[vmem],
        out_specs=vmem,
        compiler_params=pltpu.CompilerParams(vmem_limit_bytes=32 * 2**20),
    )(sums)


def solution(mesh):
    grid = Mesh(mesh.devices.reshape(8, 8, 8, 2), ("z", "y", "x", "c"))
    return jax.shard_map(
        body,
        mesh=grid,
        in_specs=(P(("z", "y"), ("x", "c")), P(("z", "y"), ("x", "c")), P()),
        out_specs=P(("x", "c"), None, None),
        check_vma=False,
    )
```

```python
import jax
import jax.numpy as jnp
import numpy as np
from jax import lax
from jax.experimental import pallas as pl
from jax.experimental.pallas import tpu as pltpu
from jax.sharding import Mesh, PartitionSpec as P

KV_RANK = 512
V_DIM = 128
ITERS = 5

epsilon = 1e-07
coef_one = 3.4445
coef_two = -4.775
coef_three = 2.0315

SIDES = (8, 8, 8, 2)
AXES = ("z", "y", "x", "c")
NN = (((1,), (0,)), ((), ()))
NT = (((1,), (1,)), ((), ()))

VMEM = pl.BlockSpec(memory_space=pltpu.VMEM)
SMEM = pl.BlockSpec(memory_space=pltpu.SMEM)


def ring_groups(first_axis):
    index = np.arange(np.prod(SIDES)).reshape(SIDES)
    rings = []
    for core in range(2):
        axis = first_axis if core == 0 else 1 - first_axis
        rings += np.moveaxis(index[..., core], axis, -1).reshape(-1, SIDES[axis]).tolist()
    return rings


def exchange(blocks, groups):
    return lax.all_to_all(blocks, AXES, 0, 0, axis_index_groups=groups, tiled=True)


def run_kernel(kernel, shape, specs, *operands, flops=0):
    size = 2 * int(np.prod(shape))
    return pl.pallas_call(
        kernel,
        out_shape=jax.ShapeDtypeStruct(shape, jnp.bfloat16),
        in_specs=specs,
        out_specs=VMEM,
        cost_estimate=pl.CostEstimate(flops=flops, bytes_accessed=2 * size, transcendentals=0),
        compiler_params=pltpu.CompilerParams(vmem_limit_bytes=32 * 2**20),
    )(*operands)


def masked_product(lengths_ref, latent_ref, grad_ref):
    own_length = lengths_ref[lax.axis_index(("z", "y"))]
    slot = lax.broadcasted_iota(jnp.int32, latent_ref.shape, 1)
    live = jnp.where(slot < own_length, latent_ref[...], jnp.zeros((), jnp.bfloat16))
    sums = lax.dot_general(live, grad_ref[...], NN, preferred_element_type=jnp.float32)
    return sums.astype(jnp.bfloat16)


def own_kernel(lengths_ref, latent_ref, grad_ref, out_ref):
    sums = masked_product(lengths_ref, latent_ref, grad_ref)
    for head in range(out_ref.shape[0]):
        out_ref[head] = sums[:, head * V_DIM : (head + 1) * V_DIM]


def other_kernel(lengths_ref, latent_ref, grad_ref, own_ref, out_ref):
    heads = own_ref.shape[0]
    out_ref[:heads] = own_ref[...]
    sums = masked_product(lengths_ref, latent_ref, grad_ref)
    for head in range(heads):
        out_ref[heads + head] = sums[:, head * V_DIM : (head + 1) * V_DIM]


def total_kernel(parts_ref, out_ref):
    total = jnp.sum(parts_ref[...].astype(jnp.float32), axis=0).astype(jnp.bfloat16)
    out_ref[...] = jnp.broadcast_to(total[None], out_ref.shape)


def ortho_kernel(sums_ref, out_ref):
    heads, chips, cores, columns, _ = out_ref.shape
    core = lax.axis_index("c")
    scale = 0.2 * max(KV_RANK, V_DIM) ** 0.5
    ortho = []
    for head in range(heads):
        rows = [sums_ref[part * heads + head] for part in range(cores)]
        wide = jnp.concatenate(rows, axis=0).astype(jnp.float32)
        norm = jnp.sqrt(jnp.sum(wide * wide))
        wide = wide * (1.0 / (norm + epsilon))
        ortho.append(jnp.transpose(wide).astype(jnp.bfloat16))
    for step in range(ITERS):
        gram = [
            lax.dot_general(x, x, NT, preferred_element_type=jnp.float32).astype(jnp.bfloat16)
            for x in ortho
        ]
        squared = [lax.dot_general(a, a, NN, preferred_element_type=jnp.float32) for a in gram]
        poly = [
            (coef_two * a.astype(jnp.float32) + coef_three * s).astype(jnp.bfloat16)
            for a, s in zip(gram, squared)
        ]
        product = [
            lax.dot_general(b, x, NN, preferred_element_type=jnp.float32)
            for b, x in zip(poly, ortho)
        ]
        ortho = [
            (coef_one * x.astype(jnp.float32) + p).astype(jnp.bfloat16)
            for x, p in zip(ortho, product)
        ]
    for head in range(heads):
        wide = jnp.transpose(scale * ortho[head].astype(jnp.float32)).astype(jnp.bfloat16)
        for part in range(cores):
            owner = core if part == 0 else 1 - core
            for chip in range(chips):
                start = (part * chips + chip) * columns
                out_ref[head, chip, owner] = wide[start : start + columns]


def body(latent, value_grad, lengths):
    capacity, columns = latent.shape
    heads = value_grad.shape[1] // V_DIM
    chips, cores = lax.axis_size("x"), lax.axis_size("c")
    rows = chips * columns
    flops = 2 * rows * capacity * heads * V_DIM
    first, second = ring_groups(1), ring_groups(0)

    gathered = lax.all_gather(latent.T, "x", axis=0, tiled=True)
    swapped = lax.ppermute(gathered, "c", [(0, 1), (1, 0)])
    specs = [SMEM, VMEM, VMEM]
    own = run_kernel(
        own_kernel, (heads, rows, V_DIM), specs, lengths, gathered, value_grad, flops=flops
    )
    blocks = run_kernel(
        other_kernel,
        (cores * heads, rows, V_DIM),
        specs + [VMEM],
        lengths,
        swapped,
        value_grad,
        own,
        flops=flops,
    )
    parts = exchange(blocks, first)
    parts = exchange(run_kernel(total_kernel, parts.shape, [VMEM], parts), second)
    sums = exchange(run_kernel(total_kernel, parts.shape, [VMEM], parts), first)
    update = run_kernel(ortho_kernel, (heads, chips, cores, columns, V_DIM), [VMEM], sums)
    return update.reshape(heads, KV_RANK, V_DIM)


def solution(mesh):
    return jax.shard_map(
        body,
        mesh=Mesh(mesh.devices.reshape(SIDES), AXES),
        in_specs=(P(("z", "y"), ("x", "c")), P(("z", "y"), ("x", "c")), P()),
        out_specs=P(("x", "c"), None, None),
        check_vma=False,
    )
```

```python
import jax
import jax.numpy as jnp
import numpy as np
from jax import lax
from jax.experimental import pallas as pl
from jax.experimental.pallas import tpu as pltpu
from jax.sharding import Mesh, PartitionSpec as P

KV_RANK = 512
V_DIM = 128
ITERS = 5

epsilon = 1e-07
coef_one = 3.4445
coef_two = -4.775
coef_three = 2.0315

LANES = 128
LATENT_MAX = 16.0
HEADROOM = 10.0

SIDES = (8, 8, 8, 2)
AXES = ("z", "y", "x", "c")
NN = (((1,), (0,)), ((), ()))
NT = (((1,), (1,)), ((), ()))

VMEM = pl.BlockSpec(memory_space=pltpu.VMEM)
SMEM = pl.BlockSpec(memory_space=pltpu.SMEM)


def ring_groups(first_axis):
    index = np.arange(np.prod(SIDES)).reshape(SIDES)
    rings = []
    for core in range(2):
        axis = first_axis if core == 0 else 1 - first_axis
        rings += np.moveaxis(index[..., core], axis, -1).reshape(-1, SIDES[axis]).tolist()
    return rings


def exchange(blocks, groups):
    return lax.all_to_all(blocks, AXES, 0, 0, axis_index_groups=groups, tiled=True)


def run_kernel(kernel, shape, specs, *operands):
    return pl.pallas_call(
        kernel,
        out_shape=jax.ShapeDtypeStruct(shape, jnp.bfloat16),
        in_specs=specs,
        out_specs=VMEM,
        compiler_params=pltpu.CompilerParams(vmem_limit_bytes=32 * 2**20),
    )(*operands)


def encode_kernel(lengths_ref, latent_ref, out_ref):
    columns, capacity = latent_ref.shape
    own_length = lengths_ref[lax.axis_index(("z", "y"))]
    slot = lax.broadcasted_iota(jnp.int32, (columns, capacity), 1)
    live = jnp.where(slot < own_length, latent_ref[...].astype(jnp.float32), 0.0)
    largest = jnp.max(jnp.abs(live), axis=1, keepdims=True)
    shift = jnp.floor(jnp.log(LATENT_MAX / largest) * (1.0 / np.log(2.0)))
    shift = jnp.clip(shift, 0.0, 110.0)
    scaled = live * jnp.exp2(shift + HEADROOM)
    out_ref[:, :capacity] = scaled.astype(jnp.bfloat16)
    out_ref[:, capacity:] = jnp.broadcast_to(shift, (columns, LANES)).astype(jnp.bfloat16)


def partial_kernel(latent_ref, grad_ref, out_ref):
    capacity = grad_ref.shape[0]
    blocks, rows, _ = out_ref.shape
    heads = grad_ref.shape[1] // V_DIM
    for part in range(blocks // heads):
        here = slice(part * rows, (part + 1) * rows)
        sums = lax.dot_general(
            latent_ref[here, :capacity], grad_ref[...], NN, preferred_element_type=jnp.float32
        )
        shift = latent_ref[here, capacity:].astype(jnp.float32)[:, :1]
        sums = (sums * jnp.exp2(-HEADROOM - shift)).astype(jnp.bfloat16)
        for head in range(heads):
            out_ref[part * heads + head] = sums[:, head * V_DIM : (head + 1) * V_DIM]


def total_kernel(parts_ref, out_ref):
    total = jnp.sum(parts_ref[...].astype(jnp.float32), axis=0).astype(jnp.bfloat16)
    out_ref[...] = jnp.broadcast_to(total[None], out_ref.shape)


def ortho_kernel(sums_ref, out_ref):
    heads = out_ref.shape[0]
    parts = sums_ref.shape[0] // heads
    scale = 0.2 * max(KV_RANK, V_DIM) ** 0.5
    ortho = []
    for head in range(heads):
        rows = [sums_ref[part * heads + head] for part in range(parts)]
        wide = jnp.concatenate(rows, axis=0).astype(jnp.float32)
        norm = jnp.sqrt(jnp.sum(wide * wide))
        wide = wide * (1.0 / (norm + epsilon))
        ortho.append(jnp.transpose(wide).astype(jnp.bfloat16))
    for step in range(ITERS):
        gram = [
            lax.dot_general(x, x, NT, preferred_element_type=jnp.float32).astype(jnp.bfloat16)
            for x in ortho
        ]
        squared = [lax.dot_general(a, a, NN, preferred_element_type=jnp.float32) for a in gram]
        poly = [
            (coef_two * a.astype(jnp.float32) + coef_three * s).astype(jnp.bfloat16)
            for a, s in zip(gram, squared)
        ]
        product = [
            lax.dot_general(b, x, NN, preferred_element_type=jnp.float32)
            for b, x in zip(poly, ortho)
        ]
        ortho = [
            (coef_one * x.astype(jnp.float32) + p).astype(jnp.bfloat16)
            for x, p in zip(ortho, product)
        ]
    for head in range(heads):
        out_ref[head] = jnp.transpose(scale * ortho[head].astype(jnp.float32)).astype(jnp.bfloat16)


def body(latent, value_grad, lengths):
    capacity, columns = latent.shape
    heads = value_grad.shape[1] // V_DIM
    first, second = ring_groups(1), ring_groups(0)

    coded = run_kernel(encode_kernel, (columns, capacity + LANES), [SMEM, VMEM], lengths, latent.T)
    gathered = lax.all_gather(coded.astype(jnp.float16), ("x", "c"), axis=0, tiled=True)
    blocks = run_kernel(
        partial_kernel,
        (2 * heads, KV_RANK // 2, V_DIM),
        [VMEM, VMEM],
        gathered.astype(jnp.bfloat16),
        value_grad,
    )
    parts = exchange(blocks, first)
    parts = exchange(run_kernel(total_kernel, parts.shape, [VMEM], parts), second)
    sums = exchange(run_kernel(total_kernel, parts.shape, [VMEM], parts), first)
    return run_kernel(ortho_kernel, (heads, KV_RANK, V_DIM), [VMEM], sums)


def solution(mesh):
    return jax.shard_map(
        body,
        mesh=Mesh(mesh.devices.reshape(SIDES), AXES),
        in_specs=(P(("z", "y"), ("x", "c")), P(("z", "y"), ("x", "c")), P()),
        out_specs=P(("x", "c"), None, None),
        check_vma=False,
    )
```

```python
import jax
import jax.numpy as jnp
import numpy as np
from jax import lax
from jax.experimental import pallas as pl
from jax.experimental.pallas import tpu as pltpu
from jax.sharding import Mesh, PartitionSpec as P

KV_RANK = 512
V_DIM = 128
ITERS = 5

epsilon = 1e-07
coef_one = 3.4445
coef_two = -4.775
coef_three = 2.0315

LANES = 128
LATENT_MAX = 16.0
HEADROOM = 10.0

SIDES = (8, 8, 8, 2)
AXES = ("z", "y", "x", "c")
NN = (((1,), (0,)), ((), ()))
NT = (((1,), (1,)), ((), ()))

VMEM = pl.BlockSpec(memory_space=pltpu.VMEM)
SMEM = pl.BlockSpec(memory_space=pltpu.SMEM)


ORDER = [0, 4, 3, 7, 1, 5, 2, 6]
PAIR = 1


def stage_groups():
    index = np.arange(np.prod(SIDES)).reshape(SIDES)
    wide, narrow = [], []
    for core in range(2):
        plane = index[..., core] if core == 0 else index[..., core].swapaxes(0, 1)
        for column in range(SIDES[2]):
            for start in range(0, SIDES[0], PAIR):
                ring = plane[start : start + PAIR, ORDER, column]
                wide.append(ring.reshape(-1).tolist())
            for place in range(SIDES[1]):
                for start in range(PAIR):
                    narrow.append(plane[start::PAIR, place, column][ORDER].tolist())
    return wide, narrow


def exchange(blocks, groups):
    return lax.all_to_all(blocks, AXES, 0, 0, axis_index_groups=groups, tiled=True)


def run_kernel(kernel, shape, specs, *operands):
    return pl.pallas_call(
        kernel,
        out_shape=jax.ShapeDtypeStruct(shape, jnp.bfloat16),
        in_specs=specs,
        out_specs=VMEM,
        compiler_params=pltpu.CompilerParams(vmem_limit_bytes=32 * 2**20),
    )(*operands)


def encode_kernel(lengths_ref, latent_ref, out_ref):
    columns, capacity = latent_ref.shape
    own_length = lengths_ref[lax.axis_index(("z", "y"))]
    slot = lax.broadcasted_iota(jnp.int32, (columns, capacity), 1)
    live = jnp.where(slot < own_length, latent_ref[...].astype(jnp.float32), 0.0)
    largest = jnp.max(jnp.abs(live), axis=1, keepdims=True)
    shift = jnp.floor(jnp.log(LATENT_MAX / largest) * (1.0 / np.log(2.0)))
    shift = jnp.clip(shift, 0.0, 110.0)
    scaled = live * jnp.exp2(shift + HEADROOM)
    out_ref[:, :capacity] = scaled.astype(jnp.bfloat16)
    out_ref[:, capacity:] = jnp.broadcast_to(shift, (columns, LANES)).astype(jnp.bfloat16)


def partial_kernel(latent_ref, grad_ref, out_ref):
    capacity = grad_ref.shape[0]
    blocks, rows, _ = out_ref.shape
    heads = grad_ref.shape[1] // V_DIM
    for part in range(blocks // heads):
        here = slice(part * rows, (part + 1) * rows)
        coded = latent_ref[here, :capacity]
        sums = lax.dot_general(coded, grad_ref[...], NN, preferred_element_type=jnp.float32)
        shift = latent_ref[here, capacity:].astype(jnp.float32)[:, :1]
        sums = (sums * jnp.exp2(-HEADROOM - shift)).astype(jnp.bfloat16)
        for head in range(heads):
            out_ref[part * heads + head] = sums[:, head * V_DIM : (head + 1) * V_DIM]


def total_kernel(parts_ref, out_ref):
    total = jnp.sum(parts_ref[...].astype(jnp.float32), axis=0).astype(jnp.bfloat16)
    out_ref[...] = jnp.broadcast_to(total[None], out_ref.shape)


def ortho_kernel(sums_ref, out_ref):
    heads = out_ref.shape[0]
    parts = sums_ref.shape[0] // heads
    scale = 0.2 * max(KV_RANK, V_DIM) ** 0.5
    sums = [
        jnp.concatenate([sums_ref[part * heads + head] for part in range(parts)], axis=0)
        for head in range(heads)
    ]
    turned = [jnp.transpose(g) for g in sums]
    gram = [lax.dot_general(t, t, NT, preferred_element_type=jnp.float32) for t in turned]
    wide = [g.astype(jnp.float32) for g in sums]
    inverse = [1.0 / (jnp.sqrt(jnp.sum(w * w)) + epsilon) for w in wide]
    gram = [(a * (i * i)).astype(jnp.bfloat16) for a, i in zip(gram, inverse)]
    ortho = [(t.astype(jnp.float32) * i).astype(jnp.bfloat16) for t, i in zip(turned, inverse)]
    for step in range(ITERS):
        if step:
            gram = [
                lax.dot_general(x, x, NT, preferred_element_type=jnp.float32).astype(jnp.bfloat16)
                for x in ortho
            ]
        squared = [lax.dot_general(a, a, NN, preferred_element_type=jnp.float32) for a in gram]
        poly = [
            (coef_two * a.astype(jnp.float32) + coef_three * s).astype(jnp.bfloat16)
            for a, s in zip(gram, squared)
        ]
        product = [
            lax.dot_general(b, x, NN, preferred_element_type=jnp.float32)
            for b, x in zip(poly, ortho)
        ]
        ortho = [
            (coef_one * x.astype(jnp.float32) + p).astype(jnp.bfloat16)
            for x, p in zip(ortho, product)
        ]
    for head in range(heads):
        out_ref[head] = jnp.transpose(scale * ortho[head].astype(jnp.float32)).astype(jnp.bfloat16)


def body(latent, value_grad, lengths):
    capacity, columns = latent.shape
    heads = value_grad.shape[1] // V_DIM
    wide, narrow = stage_groups()

    coded = run_kernel(encode_kernel, (columns, capacity + LANES), [SMEM, VMEM], lengths, latent.T)
    gathered = lax.all_gather(coded.astype(jnp.float16), ("x", "c"), axis=0, tiled=True)
    members, others = len(wide[0]), len(narrow[0])
    block = (KV_RANK * heads // members, V_DIM)
    blocks = run_kernel(
        partial_kernel,
        (members, *block),
        [VMEM, VMEM],
        gathered.astype(jnp.bfloat16),
        value_grad,
    )
    parts = exchange(blocks, wide)
    parts = exchange(run_kernel(total_kernel, (others, *block), [VMEM], parts), narrow)
    sums = exchange(run_kernel(total_kernel, (members, *block), [VMEM], parts), wide)
    return run_kernel(ortho_kernel, (heads, KV_RANK, V_DIM), [VMEM], sums)


def solution(mesh):
    return jax.shard_map(
        body,
        mesh=Mesh(mesh.devices.reshape(SIDES), AXES),
        in_specs=(P(("z", "y"), ("x", "c")), P(("z", "y"), ("x", "c")), P()),
        out_specs=P(("x", "c"), None, None),
        check_vma=False,
    )
```

```python
import jax
import jax.numpy as jnp
import numpy as np
from jax import lax
from jax.experimental import pallas as pl
from jax.experimental.pallas import tpu as pltpu
from jax.sharding import Mesh, PartitionSpec as P

KV_RANK = 512
V_DIM = 128
ITERS = 5

epsilon = 1e-07
coef_one = 3.4445
coef_two = -4.775
coef_three = 2.0315

LANES = 128
LATENT_MAX = 16.0
HEADROOM = 10.0

SIDES = (8, 8, 8, 2)
AXES = ("z", "y", "x", "c")
NN = (((1,), (0,)), ((), ()))
NT = (((1,), (1,)), ((), ()))

VMEM = pl.BlockSpec(memory_space=pltpu.VMEM)
SMEM = pl.BlockSpec(memory_space=pltpu.SMEM)


ORDER = [0, 4, 3, 7, 1, 5, 2, 6]
PAIR = 1


def stage_groups():
    index = np.arange(np.prod(SIDES)).reshape(SIDES)
    wide, narrow = [], []
    for core in range(2):
        plane = index[..., core] if core == 0 else index[..., core].swapaxes(0, 1)
        for column in range(SIDES[2]):
            for start in range(0, SIDES[0], PAIR):
                ring = plane[start : start + PAIR, ORDER, column]
                wide.append(ring.reshape(-1).tolist())
            for place in range(SIDES[1]):
                for start in range(PAIR):
                    narrow.append(plane[start::PAIR, place, column][ORDER].tolist())
    return wide, narrow


def exchange(blocks, groups):
    return lax.all_to_all(blocks, AXES, 0, 0, axis_index_groups=groups, tiled=True)


def run_kernel(kernel, shape, specs, *operands):
    return pl.pallas_call(
        kernel,
        out_shape=jax.ShapeDtypeStruct(shape, jnp.bfloat16),
        in_specs=specs,
        out_specs=VMEM,
        compiler_params=pltpu.CompilerParams(vmem_limit_bytes=32 * 2**20),
    )(*operands)


def encode_kernel(lengths_ref, latent_ref, out_ref):
    columns, capacity = latent_ref.shape
    own_length = lengths_ref[lax.axis_index(("z", "y"))]
    slot = lax.broadcasted_iota(jnp.int32, (columns, capacity), 1)
    live = jnp.where(slot < own_length, latent_ref[...].astype(jnp.float32), 0.0)
    largest = jnp.max(jnp.abs(live), axis=1, keepdims=True)
    shift = jnp.floor(jnp.log(LATENT_MAX / largest) * (1.0 / np.log(2.0)))
    shift = jnp.clip(shift, 0.0, 110.0)
    scaled = live * jnp.exp2(shift + HEADROOM)
    out_ref[:, :capacity] = scaled.astype(jnp.bfloat16)
    out_ref[:, capacity:] = jnp.broadcast_to(shift, (columns, LANES)).astype(jnp.bfloat16)


def partial_kernel(latent_ref, grad_ref, out_ref):
    capacity = grad_ref.shape[0]
    blocks, rows, _ = out_ref.shape
    heads = grad_ref.shape[1] // V_DIM
    for part in range(blocks // heads):
        here = slice(part * rows, (part + 1) * rows)
        coded = latent_ref[here, :capacity]
        sums = lax.dot_general(coded, grad_ref[...], NN, preferred_element_type=jnp.float32)
        shift = latent_ref[here, capacity:].astype(jnp.float32)[:, :1]
        sums = (sums * jnp.exp2(-HEADROOM - shift)).astype(jnp.bfloat16)
        for head in range(heads):
            out_ref[part * heads + head] = sums[:, head * V_DIM : (head + 1) * V_DIM]


def total_kernel(parts_ref, out_ref):
    total = jnp.sum(parts_ref[...].astype(jnp.float32), axis=0).astype(jnp.bfloat16)
    out_ref[...] = jnp.broadcast_to(total[None], out_ref.shape)


def ortho_kernel(sums_ref, out_hbm, out_ref, sent):
    heads = out_ref.shape[0]
    parts = sums_ref.shape[0] // heads
    scale = 0.2 * max(KV_RANK, V_DIM) ** 0.5
    sums = [
        jnp.concatenate([sums_ref[part * heads + head] for part in range(parts)], axis=0)
        for head in range(heads)
    ]
    turned = [jnp.transpose(g) for g in sums]
    gram = [lax.dot_general(t, t, NT, preferred_element_type=jnp.float32) for t in turned]
    wide = [g.astype(jnp.float32) for g in sums]
    inverse = [1.0 / (jnp.sqrt(jnp.sum(w * w)) + epsilon) for w in wide]
    gram = [(a * (i * i)).astype(jnp.bfloat16) for a, i in zip(gram, inverse)]
    ortho = [(t.astype(jnp.float32) * i).astype(jnp.bfloat16) for t, i in zip(turned, inverse)]
    for step in range(ITERS):
        if step:
            gram = [
                lax.dot_general(x, x, NT, preferred_element_type=jnp.float32).astype(jnp.bfloat16)
                for x in ortho
            ]
        squared = [lax.dot_general(a, a, NN, preferred_element_type=jnp.float32) for a in gram]
        poly = [
            (coef_two * a.astype(jnp.float32) + coef_three * s).astype(jnp.bfloat16)
            for a, s in zip(gram, squared)
        ]
        product = [
            lax.dot_general(b, x, NN, preferred_element_type=jnp.float32)
            for b, x in zip(poly, ortho)
        ]
        ortho = [
            (coef_one * x.astype(jnp.float32) + p).astype(jnp.bfloat16)
            for x, p in zip(ortho, product)
        ]
    copies = []
    for head in range(heads):
        out_ref[head] = jnp.transpose(scale * ortho[head].astype(jnp.float32)).astype(jnp.bfloat16)
        copies.append(pltpu.make_async_copy(out_ref.at[head], out_hbm.at[head], sent.at[head]))
        copies[head].start()
    for copy in copies:
        copy.wait()


def body(latent, value_grad, lengths):
    capacity, columns = latent.shape
    heads = value_grad.shape[1] // V_DIM
    wide, narrow = stage_groups()

    coded = run_kernel(encode_kernel, (columns, capacity + LANES), [SMEM, VMEM], lengths, latent.T)
    gathered = lax.all_gather(coded.astype(jnp.float16), ("x", "c"), axis=0, tiled=True)
    members, others = len(wide[0]), len(narrow[0])
    block = (KV_RANK * heads // members, V_DIM)
    blocks = run_kernel(
        partial_kernel,
        (members, *block),
        [VMEM, VMEM],
        gathered.astype(jnp.bfloat16),
        value_grad,
    )
    parts = exchange(blocks, wide)
    parts = exchange(run_kernel(total_kernel, (others, *block), [VMEM], parts), narrow)
    sums = exchange(run_kernel(total_kernel, (members, *block), [VMEM], parts), wide)
    shape = (heads, KV_RANK, V_DIM)
    return pl.pallas_call(
        ortho_kernel,
        out_shape=jax.ShapeDtypeStruct(shape, jnp.bfloat16),
        in_specs=[VMEM],
        out_specs=pl.BlockSpec(memory_space=pl.ANY),
        scratch_shapes=[pltpu.VMEM(shape, jnp.bfloat16), pltpu.SemaphoreType.DMA((heads,))],
        compiler_params=pltpu.CompilerParams(vmem_limit_bytes=32 * 2**20),
    )(sums)


def solution(mesh):
    return jax.shard_map(
        body,
        mesh=Mesh(mesh.devices.reshape(SIDES), AXES),
        in_specs=(P(("z", "y"), ("x", "c")), P(("z", "y"), ("x", "c")), P()),
        out_specs=P(("x", "c"), None, None),
        check_vma=False,
    )
```

```python
import jax
import jax.numpy as jnp
import numpy as np
from jax import lax
from jax.experimental import pallas as pl
from jax.experimental.pallas import tpu as pltpu
from jax.sharding import Mesh, PartitionSpec as P

KV_RANK = 512
V_DIM = 128
ITERS = 5

epsilon = 1e-07
coef_one = 3.4445
coef_two = -4.775
coef_three = 2.0315

LANES = 128
LATENT_MAX = 16.0
HEADROOM = 10.0

SIDES = (8, 8, 8, 2)
AXES = ("z", "y", "x", "c")
NN = (((1,), (0,)), ((), ()))
NT = (((1,), (1,)), ((), ()))

VMEM = pl.BlockSpec(memory_space=pltpu.VMEM)
SMEM = pl.BlockSpec(memory_space=pltpu.SMEM)


SCATTER = [0, 4, 3, 7, 1, 5, 2, 6]
ACROSS = [0, 4, 3, 5, 2, 6, 1, 7]
GATHER = [0, 4, 3, 7, 1, 5, 2, 6]


def ring_groups(first, order):
    index = np.arange(np.prod(SIDES)).reshape(SIDES)
    rings = []
    for core in range(2):
        axis = 1 - core if first else core
        lines = np.moveaxis(index[..., core], axis, -1).reshape(-1, SIDES[axis])
        rings += lines[:, order].tolist()
    return rings


def exchange(blocks, groups):
    return lax.all_to_all(blocks, AXES, 0, 0, axis_index_groups=groups, tiled=True)


def run_kernel(kernel, shape, specs, *operands):
    return pl.pallas_call(
        kernel,
        out_shape=jax.ShapeDtypeStruct(shape, jnp.bfloat16),
        in_specs=specs,
        out_specs=VMEM,
        compiler_params=pltpu.CompilerParams(vmem_limit_bytes=32 * 2**20),
    )(*operands)


def encode_kernel(lengths_ref, latent_ref, out_ref):
    columns, capacity = latent_ref.shape
    own_length = lengths_ref[lax.axis_index(("z", "y"))]
    slot = lax.broadcasted_iota(jnp.int32, (columns, capacity), 1)
    live = jnp.where(slot < own_length, latent_ref[...].astype(jnp.float32), 0.0)
    largest = jnp.max(jnp.abs(live), axis=1, keepdims=True)
    shift = jnp.floor(jnp.log(LATENT_MAX / largest) * (1.0 / np.log(2.0)))
    shift = jnp.clip(shift, 0.0, 110.0)
    scaled = live * jnp.exp2(shift + HEADROOM)
    out_ref[:, :capacity] = scaled.astype(jnp.bfloat16)
    out_ref[:, capacity:] = jnp.broadcast_to(shift, (columns, LANES)).astype(jnp.bfloat16)


def partial_kernel(latent_ref, grad_ref, out_ref):
    capacity = grad_ref.shape[0]
    blocks, rows, _ = out_ref.shape
    heads = grad_ref.shape[1] // V_DIM
    for part in range(blocks // heads):
        here = slice(part * rows, (part + 1) * rows)
        coded = latent_ref[here, :capacity]
        sums = lax.dot_general(coded, grad_ref[...], NN, preferred_element_type=jnp.float32)
        shift = latent_ref[here, capacity:].astype(jnp.float32)[:, :1]
        sums = (sums * jnp.exp2(-HEADROOM - shift)).astype(jnp.bfloat16)
        for head in range(heads):
            out_ref[part * heads + head] = sums[:, head * V_DIM : (head + 1) * V_DIM]


def total_kernel(parts_ref, out_ref):
    total = jnp.sum(parts_ref[...].astype(jnp.float32), axis=0).astype(jnp.bfloat16)
    out_ref[...] = jnp.broadcast_to(total[None], out_ref.shape)


def ortho_kernel(sums_ref, out_ref):
    heads = out_ref.shape[0]
    parts = sums_ref.shape[0] // heads
    place = [GATHER.index(device) for device in SCATTER]
    scale = 0.2 * max(KV_RANK, V_DIM) ** 0.5
    sums = [
        jnp.concatenate([sums_ref[place[part * heads + head]] for part in range(parts)], axis=0)
        for head in range(heads)
    ]
    turned = [jnp.transpose(g) for g in sums]
    gram = [lax.dot_general(t, t, NT, preferred_element_type=jnp.float32) for t in turned]
    wide = [g.astype(jnp.float32) for g in sums]
    inverse = [1.0 / (jnp.sqrt(jnp.sum(w * w)) + epsilon) for w in wide]
    gram = [(a * (i * i)).astype(jnp.bfloat16) for a, i in zip(gram, inverse)]
    ortho = [(t.astype(jnp.float32) * i).astype(jnp.bfloat16) for t, i in zip(turned, inverse)]
    for step in range(ITERS):
        if step:
            gram = [
                lax.dot_general(x, x, NT, preferred_element_type=jnp.float32).astype(jnp.bfloat16)
                for x in ortho
            ]
        squared = [lax.dot_general(a, a, NN, preferred_element_type=jnp.float32) for a in gram]
        poly = [
            (coef_two * a.astype(jnp.float32) + coef_three * s).astype(jnp.bfloat16)
            for a, s in zip(gram, squared)
        ]
        product = [
            lax.dot_general(b, x, NN, preferred_element_type=jnp.float32)
            for b, x in zip(poly, ortho)
        ]
        ortho = [
            (coef_one * x.astype(jnp.float32) + p).astype(jnp.bfloat16)
            for x, p in zip(ortho, product)
        ]
    for head in range(heads):
        out_ref[head] = jnp.transpose(scale * ortho[head].astype(jnp.float32)).astype(jnp.bfloat16)


def body(latent, value_grad, lengths):
    capacity, columns = latent.shape
    heads = value_grad.shape[1] // V_DIM
    scatter = ring_groups(True, SCATTER)
    across = ring_groups(False, ACROSS)
    gather = ring_groups(True, GATHER)

    coded = run_kernel(encode_kernel, (columns, capacity + LANES), [SMEM, VMEM], lengths, latent.T)
    gathered = lax.all_gather(coded.astype(jnp.float16), ("x", "c"), axis=0, tiled=True)
    members = len(SCATTER)
    block = (KV_RANK * heads // members, V_DIM)
    blocks = run_kernel(
        partial_kernel,
        (members, *block),
        [VMEM, VMEM],
        gathered.astype(jnp.bfloat16),
        value_grad,
    )
    parts = exchange(blocks, scatter)
    parts = exchange(run_kernel(total_kernel, parts.shape, [VMEM], parts), across)
    sums = exchange(run_kernel(total_kernel, parts.shape, [VMEM], parts), gather)
    return run_kernel(ortho_kernel, (heads, KV_RANK, V_DIM), [VMEM], sums)


def solution(mesh):
    return jax.shard_map(
        body,
        mesh=Mesh(mesh.devices.reshape(SIDES), AXES),
        in_specs=(P(("z", "y"), ("x", "c")), P(("z", "y"), ("x", "c")), P()),
        out_specs=P(("x", "c"), None, None),
        check_vma=False,
    )
```
